32 devices in a mesh: lat: 8 (over z, y), lev: 4 (over x, core).
Axes of the slice: x: 2, y: 2, z: 4, core: 2. Of those that a mesh axis runs over, the one named last changes fastest.
Arguments:
- grid_old: bfloat16 [3, 4, 128, 5120], P(None, 'lev', 'lat'), may hold values from -6 to 6
- depart_offset: int32 [4, 128, 5120], P('lev', 'lat'), may hold values from -12 to 9, as said below
- interp_weights: bfloat16 [4, 4, 128, 5120], P(None, 'lev', 'lat'), may hold values from -0.25 to 0.75
- pair_order: int32 [384], replicated, may hold values from 0 to 383, each once
- legendre: bfloat16 [384, 769, 128], P(('lat', 'lev')), may hold values from -0.5 to 0.5
- helmholtz: float32 [768, 4, 4], replicated, may hold values from -3 to 3
Outputs:
- grid_new: bfloat16 [3, 4, 128, 5120], P(None, 'lev', 'lat')
The draws below stay inside these ranges and needn't reach their ends.
Inputs may be any that keep to these rules, and one draw needn't show every extreme that they name: `depart_offset`: in the rows of each index of lat, every offset lies in -w to w - 3 for that band's width w, which is at most 12; some band has width 12 and reaches both ends. `pair_order`: A permutation of the wavenumber pairs.
All inputs are finite; a program needn't handle non-finite values.
Results may differ from the reference program's by a relative error of at most 0.017.
Values may be sent and summed in bfloat16 or wider, within the bound.
A program may use at most 64 MiB of HBM per device.

```python
import math
import jax
import jax.numpy as jnp
from jax import lax

NLON = 5120
M = 768
HMAX = 12
FIELDS = 3
ROWS_DEV = 16
LATITUDE_ROWS = 128
LEVELS = 4
WAVE_PAIR_TOTAL = 384
SLOTS_PER_PAIR = 769


def draw_depart_offset(key, part):
    band_total = LATITUDE_ROWS // ROWS_DEV
    band_width = jax.random.randint(jax.random.fold_in(key, 11), (band_total,), 3, HMAX + 1)
    chosen_band = jax.random.randint(jax.random.fold_in(key, 12), (), 0, band_total)
    band_width = band_width.at[chosen_band].set(HMAX)
    row_width = jnp.repeat(band_width, ROWS_DEV, total_repeat_length=LATITUDE_ROWS)
    lower_bound = -row_width[None, :, None]
    upper_bound = row_width[None, :, None] - 2
    offsets = jax.random.randint(jax.random.fold_in(key, 13), (LEVELS, LATITUDE_ROWS, NLON), lower_bound, upper_bound)
    first_row = chosen_band * ROWS_DEV
    offsets = offsets.at[0, first_row, 0].set(-HMAX)
    offsets = offsets.at[0, first_row + 1, 0].set(HMAX - 3)
    return offsets.astype(jnp.int32)


def steps_of(stream_key, shape, split, least, high):
    loudness = 1.0
    for dim, parts in split:
        draws = jax.random.uniform(jax.random.fold_in(jax.random.fold_in(stream_key, 6), dim), (parts,), jnp.float32, least / len(split), high / len(split))
        loudness = loudness * jnp.repeat(jnp.exp(draws), shape[dim] // parts).reshape((-1,) + (1,) * (len(shape) - 1 - dim))
    return loudness


def centred(stream_key, dims, deviation, bound, pieces=(), kind=jnp.bfloat16):
    entries = jax.random.normal(stream_key, dims, jnp.float32) * deviation
    if len(pieces) > 0:
        entries = steps_of(stream_key, dims, pieces, -0.22, 0.18) * entries
    return jnp.clip(entries, min=-bound, max=bound).astype(kind)


def setup_inputs(seed: int = 0) -> dict:
    arg_keys = jax.random.split(jax.random.key(seed), 7)
    grid_old = centred(arg_keys[0], (FIELDS, LEVELS, LATITUDE_ROWS, NLON), 1.0, 6.0, ((1, 4), (2, 8)))
    depart_offset = draw_depart_offset(jax.random.fold_in(arg_keys[6], 71), 0)
    interp_weights = jnp.clip(-0.25 + 1.0 * jax.random.uniform(arg_keys[2], (4, LEVELS, LATITUDE_ROWS, NLON), jnp.float32) ** steps_of(arg_keys[2], (4, LEVELS, LATITUDE_ROWS, NLON), ((1, 4), (2, 8)), -0.2, 0.2), -0.25, 0.75).astype(jnp.bfloat16)
    pair_order = jax.random.permutation(arg_keys[3], WAVE_PAIR_TOTAL).astype(jnp.int32)
    legendre = centred(arg_keys[4], (WAVE_PAIR_TOTAL, SLOTS_PER_PAIR, LATITUDE_ROWS), LATITUDE_ROWS ** -0.5, 0.5, ((0, 32),))
    helmholtz = centred(arg_keys[5], (M, LEVELS, LEVELS), LEVELS ** -0.5, 3.0, (), jnp.float32)
    return dict(grid_old=grid_old, depart_offset=depart_offset, interp_weights=interp_weights, pair_order=pair_order, legendre=legendre, helmholtz=helmholtz)


def reference(grid_old, depart_offset, interp_weights, pair_order, legendre, helmholtz):
    padded = jnp.pad(grid_old, ((0, 0), (0, 0), (HMAX, HMAX), (0, 0)))
    row_start = jnp.arange(LATITUDE_ROWS, dtype=jnp.int32)[None, :, None] + HMAX + depart_offset
    summed = jnp.zeros(grid_old.shape, jnp.float32)
    for offset_term in range(4):
        row_index = jnp.broadcast_to((row_start + offset_term)[None], grid_old.shape)
        picked = jnp.take_along_axis(padded, row_index, axis=2)
        summed = summed + interp_weights[offset_term].astype(jnp.float32)[None] * picked.astype(jnp.float32)
    arrival = summed.astype(jnp.bfloat16)
    scale_factor = 1.0 / math.sqrt(NLON)
    spectrum = jnp.fft.rfft(arrival.astype(jnp.float32), axis=-1)[..., :M]
    fourier_real = (jnp.real(spectrum) * scale_factor).astype(jnp.bfloat16)
    fourier_imag = (jnp.imag(spectrum) * scale_factor).astype(jnp.bfloat16)
    fourier = jnp.stack([fourier_real, fourier_imag], axis=0)
    coefficient_axis = jnp.arange(SLOTS_PER_PAIR, dtype=jnp.int32)

    def per_slot(packed):
        table, pair_index = packed
        first_wave = pair_index
        partner_wavenumber = M - 1 - pair_index
        gathered = jnp.stack([jnp.take(fourier, first_wave, axis=4), jnp.take(fourier, partner_wavenumber, axis=4)], axis=0)
        table_wide = table.astype(jnp.float32)
        projected = jnp.einsum('tj,wcfvj->twcfv', table_wide, gathered.astype(jnp.float32))
        lower = coefficient_axis < M - pair_index
        lower_mask = lower[:, None, None, None]
        chosen = jnp.where(lower_mask, projected[:, 0], projected[:, 1])
        degree = jnp.where(lower, pair_index + coefficient_axis, coefficient_axis - 1).astype(jnp.int32)
        operator = jnp.take(helmholtz, degree, axis=0)
        solved = jnp.einsum('tvw,tcfw->tcfv', operator, chosen, precision=lax.Precision.HIGHEST).astype(jnp.bfloat16)
        zero_part = jnp.zeros_like(solved)
        placed = jnp.stack([jnp.where(lower_mask, solved, zero_part), jnp.where(lower_mask, zero_part, solved)], axis=1)
        returned = jnp.einsum('tj,twcfv->wcfvj', table_wide, placed.astype(jnp.float32))
        return returned.astype(jnp.bfloat16)
    backs = lax.map(per_slot, (legendre, pair_order))
    wavenumber_index = jnp.stack([pair_order, M - 1 - pair_order], axis=1).reshape(-1).astype(jnp.int32)
    natural = jnp.zeros((M, 2, FIELDS, LEVELS, LATITUDE_ROWS), jnp.bfloat16)
    natural = natural.at[wavenumber_index].set(backs.reshape(WAVE_PAIR_TOTAL * 2, 2, FIELDS, LEVELS, LATITUDE_ROWS))
    back_real = jnp.moveaxis(natural[:, 0], 0, -1).astype(jnp.float32)
    back_imag = jnp.moveaxis(natural[:, 1], 0, -1).astype(jnp.float32)
    pad_width = ((0, 0), (0, 0), (0, 0), (0, NLON // 2 + 1 - M))
    complex_back = jnp.pad(back_real, pad_width) + 1j * jnp.pad(back_imag, pad_width)
    rebuilt = jnp.fft.irfft(complex_back, n=NLON, axis=-1) * math.sqrt(NLON)
    return rebuilt.astype(jnp.bfloat16)
```

```python
import functools
import math

import jax
import jax.numpy as jnp
import numpy as np
from jax import lax
from jax.experimental import pallas as pl
from jax.experimental.pallas import tpu as pltpu
from jax.sharding import PartitionSpec as P

HMAX = 12
LANES = 128
GROUP = 8


@functools.lru_cache(maxsize=None)
def tables(lon_count, wave_count):
    quarter = lon_count // 4
    classes = [np.arange(k, wave_count, 4) for k in (0, 2)]
    odd = np.arange(1, wave_count, 2)
    column = np.arange(quarter)
    norm = 1.0 / math.sqrt(lon_count)
    built = []
    for waves in classes:
        angle = (waves[:, None] * column[None, :] % lon_count) * (2.0 * math.pi / lon_count)
        built.append(np.stack([np.cos(angle), -np.sin(angle)]) * norm)
    angle = (odd[:, None] * column[None, :] % lon_count) * (2.0 * math.pi / lon_count)
    sign = np.where(odd % 4 == 1, 1.0, -1.0)[:, None]
    cos, sin = np.cos(angle), np.sin(angle)
    real = np.concatenate([cos, -sign * sin], axis=1)
    imag = np.concatenate([-sin, -sign * cos], axis=1)
    built.append(np.stack([real, imag]) * norm)
    order = np.concatenate(classes + [odd]).astype(np.int32)
    return [t.astype(np.float32).astype(jnp.bfloat16) for t in built], order


def interp_kernel(low_ref, mid_ref, high_ref, offset_ref, weight_ref, out_ref, wide):
    fields, rows, width = mid_ref.shape
    for f in range(fields):
        for i, ref in enumerate((low_ref, mid_ref, high_ref)):
            wide[f, i * rows : (i + 1) * rows, :] = ref[f].astype(jnp.float32)

    def chunk(step, carry):
        here = pl.ds(pl.multiple_of(step * LANES, LANES), LANES)
        offset = offset_ref[:, here]
        weights = [weight_ref[k, :, here].astype(jnp.float32) for k in range(4)]
        totals = [jnp.zeros((rows, LANES), jnp.float32) for _ in range(fields)]
        picks = [offset == start for start in range(-HMAX, HMAX - 2)]
        for shift in range(-HMAX, HMAX + 1):
            coefficient = jnp.zeros((rows, LANES), jnp.float32)
            for k in range(4):
                start = shift - k
                if -HMAX <= start < HMAX - 2:
                    coefficient = jnp.where(picks[start + HMAX], weights[k], coefficient)
            for f in range(fields):
                totals[f] = totals[f] + coefficient * wide[f, pl.ds(rows + shift, rows), here]
        for f in range(fields):
            out_ref[f, :, here] = totals[f].astype(out_ref.dtype)
        return carry

    lax.fori_loop(0, width // LANES, chunk, 0)


def interpolate(low, mid, high, offset, weights):
    fields, rows, lon_count = mid.shape
    width = lon_count // 4

    def block(lead):
        return pl.BlockSpec((lead, rows, width), lambda i: (0, 0, i))

    return pl.pallas_call(
        interp_kernel,
        grid=(lon_count // width,),
        out_shape=jax.ShapeDtypeStruct(mid.shape, mid.dtype),
        in_specs=[
            block(fields),
            block(fields),
            block(fields),
            pl.BlockSpec((rows, width), lambda i: (0, i)),
            block(4),
        ],
        out_specs=block(fields),
        scratch_shapes=[pltpu.VMEM((fields, 3 * rows, width), jnp.float32)],
        compiler_params=pltpu.CompilerParams(vmem_limit_bytes=32 * 1024 * 1024),
    )(low, mid, high, offset, weights)


def spectral_kernel(wave_count, level_count, pair_ref, table_ref, shifted_ref, leg_ref, in_ref, out_ref):
    pair = pair_ref[pl.program_id(0)]
    slots = leg_ref.shape[1]
    half = level_count * GROUP
    legendre = leg_ref[0]
    projected = lax.dot_general(
        in_ref[0], legendre, (((1,), (1,)), ((), ())), preferred_element_type=jnp.float32
    )
    table = table_ref[...]
    rolled = pltpu.roll(table, table.shape[1] - pair, 1)[:, :slots]
    upper = shifted_ref[:, :slots]

    def lower_mask(rows):
        return lax.broadcasted_iota(jnp.int32, (rows, slots), 1) < wave_count - pair

    operator = jnp.where(lower_mask(level_count * level_count), rolled, upper)
    mask = lower_mask(half)
    chosen = jnp.where(mask, projected[:half], projected[half:])
    solved = []
    for v in range(level_count):
        total = jnp.zeros((GROUP, slots), jnp.float32)
        for w in range(level_count):
            row = v * level_count + w
            total = total + operator[row : row + 1] * chosen[w * GROUP : (w + 1) * GROUP]
        solved.append(total)
    solved = jnp.concatenate(solved, axis=0)
    placed = jnp.concatenate([jnp.where(mask, solved, 0.0), jnp.where(mask, 0.0, solved)], axis=0)
    returned = jnp.dot(
        placed.astype(jnp.bfloat16), legendre, preferred_element_type=jnp.float32
    )
    out_ref[0] = returned.astype(out_ref.dtype)


def spectral(pair_here, helmholtz, legendre, stacked):
    pair_local, slot_count, lat_total = legendre.shape
    wave_count, level_count, _ = helmholtz.shape
    rows = stacked.shape[1]
    span = -(-slot_count // 256) * 256
    flat = helmholtz.reshape(wave_count, level_count * level_count).T
    table = jnp.pad(flat, ((0, 0), (0, span - wave_count)))
    shifted = jnp.pad(flat, ((0, 0), (1, span - wave_count - 1)))
    whole = pl.BlockSpec(table.shape, lambda i, pair: (0, 0))
    return pl.pallas_call(
        functools.partial(spectral_kernel, wave_count, level_count),
        grid_spec=pltpu.PrefetchScalarGridSpec(
            num_scalar_prefetch=1,
            grid=(pair_local,),
            in_specs=[
                whole,
                whole,
                pl.BlockSpec((1, slot_count, lat_total), lambda i, pair: (i, 0, 0)),
                pl.BlockSpec((1, rows, lat_total), lambda i, pair: (i, 0, 0)),
            ],
            out_specs=pl.BlockSpec((1, rows, lat_total), lambda i, pair: (i, 0, 0)),
        ),
        out_shape=jax.ShapeDtypeStruct(stacked.shape, stacked.dtype),
        compiler_params=pltpu.CompilerParams(vmem_limit_bytes=32 * 1024 * 1024),
    )(pair_here, table, shifted, legendre, stacked)


def shards(grid_old, depart_offset, interp_weights, pair_order, legendre, helmholtz):
    lat_count = lax.axis_size("lat")
    lev_count = lax.axis_size("lev")
    fields, lev_local, row_count, lon_count = grid_old.shape
    pair_count = pair_order.shape[0]
    pair_local, slot_count, lat_total = legendre.shape
    wave_count = helmholtz.shape[0]
    level_count = helmholtz.shape[1]
    local = fields * lev_local * row_count
    quarter = lon_count // 4
    assert row_count >= HMAX and 2 * fields <= GROUP
    (basis0, basis2, basis_odd), order = tables(lon_count, wave_count)
    count0, count2 = basis0.shape[1], basis2.shape[1]

    forward = [(i, i + 1) for i in range(lat_count - 1)]
    backward = [(i + 1, i) for i in range(lat_count - 1)]
    low = lax.ppermute(grid_old, "lat", forward)
    high = lax.ppermute(grid_old, "lat", backward)
    arrival = jnp.stack(
        [
            interpolate(
                low[:, v], grid_old[:, v], high[:, v], depart_offset[v], interp_weights[:, v]
            )
            for v in range(lev_local)
        ],
        axis=1,
    )
    flat = arrival.reshape(local, lon_count).astype(jnp.float32)
    f0, f1, f2, f3 = [flat[:, a * quarter : (a + 1) * quarter] for a in range(4)]
    even, swing = f0 + f2, f1 + f3
    kind = jnp.bfloat16
    sum0 = (even + swing).astype(kind)
    sum2 = (even - swing).astype(kind)
    odd = jnp.concatenate([(f0 - f2).astype(kind), (f1 - f3).astype(kind)], axis=1)

    def project(basis, part):
        return lax.dot_general(
            basis, part, (((2,), (1,)), ((), ())), preferred_element_type=jnp.float32
        ).astype(kind)

    fourier = jnp.concatenate(
        [project(basis0, sum0), project(basis2, sum2), project(basis_odd, odd)], axis=1
    )
    waves = jnp.stack([pair_order, wave_count - 1 - pair_order], axis=1).reshape(-1)
    match = waves[:, None] == order[None, :]
    select = match.astype(kind)
    sent = jnp.concatenate(
        [
            jnp.dot(select, fourier[c], preferred_element_type=jnp.float32).astype(kind)
            for c in range(2)
        ],
        axis=1,
    )
    moved = lax.all_to_all(sent, ("lat", "lev"), split_axis=0, concat_axis=0, tiled=True)
    moved = moved.reshape(
        lat_count, lev_count, pair_local, 2, 2 * fields, lev_local, row_count
    )
    stacked = moved.transpose(2, 3, 1, 5, 4, 0, 6)
    stacked = stacked.reshape(pair_local, 2, level_count, 2 * fields, lat_total)
    stacked = jnp.pad(stacked, ((0, 0),) * 3 + ((0, GROUP - 2 * fields), (0, 0)))
    stacked = stacked.reshape(pair_local, 2 * level_count * GROUP, lat_total)
    holder = lax.axis_index("lat") * lev_count + lax.axis_index("lev")
    pair_here = lax.dynamic_slice_in_dim(pair_order, holder * pair_local, pair_local)
    returned = spectral(pair_here, helmholtz, legendre, stacked)
    returned = returned.reshape(pair_local, 2, level_count, GROUP, lat_total)[:, :, :, : 2 * fields]
    returned = returned.reshape(
        pair_local, 2, lev_count, lev_local, 2 * fields, lat_count, row_count
    )
    outgoing = returned.transpose(5, 2, 0, 1, 4, 3, 6).reshape(pair_count * 2, 2 * local)
    arrived = lax.all_to_all(outgoing, ("lat", "lev"), split_axis=0, concat_axis=0, tiled=True)
    gain = jnp.where(match, np.where(order == 0, 1.0, 2.0).astype(np.float32)[None, :], 0.0)
    natural = lax.dot_general(
        gain.astype(kind), arrived, (((0,), (0,)), ((), ())), preferred_element_type=jnp.float32
    ).astype(kind)

    def rebuild(basis, first):
        total = 0.0
        for c in range(2):
            rows = natural[first : first + basis.shape[1], c * local : (c + 1) * local]
            total = total + lax.dot_general(
                rows, basis[c], (((0,), (0,)), ((), ())), preferred_element_type=jnp.float32
            )
        return total

    back0 = rebuild(basis0, 0)
    back2 = rebuild(basis2, count0)
    back_odd = rebuild(basis_odd, count0 + count2)
    plus, minus = back0 + back2, back0 - back2
    left, right = back_odd[:, :quarter], back_odd[:, quarter:]
    rebuilt = jnp.concatenate([plus + left, minus + right, plus - left, minus - right], axis=1)
    return rebuilt.astype(kind).reshape(fields, lev_local, row_count, lon_count)


def solution(mesh):
    in_specs = (
        P(None, "lev", "lat", None),
        P("lev", "lat", None),
        P(None, "lev", "lat", None),
        P(),
        P(("lat", "lev"), None, None),
        P(),
    )
    out_specs = P(None, "lev", "lat", None)
    return jax.shard_map(shards, mesh=mesh, in_specs=in_specs, out_specs=out_specs, check_vma=False)
```

```python
import functools
import math

import jax
import jax.numpy as jnp
import numpy as np
from jax import lax
from jax.experimental import pallas as pl
from jax.experimental.pallas import tpu as pltpu
from jax.sharding import PartitionSpec as P

HMAX = 12
LANES = 128
GROUP = 8
EDGE = 4


@functools.lru_cache(maxsize=None)
def tables(lon_count, wave_count):
    quarter = lon_count // 4
    classes = [np.arange(k, wave_count, 4) for k in (0, 2)]
    odd = np.arange(1, wave_count, 2)
    column = np.arange(quarter)
    norm = 1.0 / math.sqrt(lon_count)
    built = []
    for waves in classes:
        angle = (waves[:, None] * column[None, :] % lon_count) * (2.0 * math.pi / lon_count)
        built.append(np.stack([np.cos(angle), -np.sin(angle)]) * norm)
    angle = (odd[:, None] * column[None, :] % lon_count) * (2.0 * math.pi / lon_count)
    sign = np.where(odd % 4 == 1, 1.0, -1.0)[:, None]
    cos, sin = np.cos(angle), np.sin(angle)
    real = np.concatenate([cos, -sign * sin], axis=1)
    imag = np.concatenate([-sin, -sign * cos], axis=1)
    built.append(np.stack([real, imag]) * norm)
    order = np.concatenate(classes + [odd]).astype(np.int32)
    return [t.astype(np.float32).astype(jnp.bfloat16) for t in built], order


def interp_kernel(low_ref, mid_ref, high_ref, offset_ref, weight_ref, out_ref, wide):
    fields, rows, width = mid_ref.shape
    for f in range(fields):
        wide[f, rows : 2 * rows, :] = mid_ref[f].astype(jnp.float32)
        for first, ref in ((rows - HMAX, low_ref), (2 * rows, high_ref)):
            for g in range(HMAX // EDGE):
                start = first + g * EDGE
                part = ref[f * (HMAX // EDGE) + g]
                wide[f, start : start + EDGE, :] = part.astype(jnp.float32)

    def chunk(step, carry):
        here = pl.ds(pl.multiple_of(step * LANES, LANES), LANES)
        offset = offset_ref[:, here]
        weights = [weight_ref[k, :, here].astype(jnp.float32) for k in range(4)]
        totals = [jnp.zeros((rows, LANES), jnp.float32) for _ in range(fields)]
        picks = [offset == start for start in range(-HMAX, HMAX - 2)]
        for shift in range(-HMAX, HMAX + 1):
            coefficient = jnp.zeros((rows, LANES), jnp.float32)
            for k in range(4):
                start = shift - k
                if -HMAX <= start < HMAX - 2:
                    coefficient = jnp.where(picks[start + HMAX], weights[k], coefficient)
            for f in range(fields):
                totals[f] = totals[f] + coefficient * wide[f, pl.ds(rows + shift, rows), here]
        for f in range(fields):
            out_ref[f, :, here] = totals[f].astype(out_ref.dtype)
        return carry

    lax.fori_loop(0, width // LANES, chunk, 0)


def interpolate(low, mid, high, offset, weights):
    fields, rows, lon_count = mid.shape
    width = lon_count // 4

    def block(lead):
        return pl.BlockSpec((lead, rows, width), lambda i: (0, 0, i))

    edge = pl.BlockSpec((low.shape[0], EDGE, width), lambda i: (0, 0, i))
    return pl.pallas_call(
        interp_kernel,
        grid=(lon_count // width,),
        out_shape=jax.ShapeDtypeStruct(mid.shape, mid.dtype),
        in_specs=[
            edge,
            block(fields),
            edge,
            pl.BlockSpec((rows, width), lambda i: (0, i)),
            block(4),
        ],
        out_specs=block(fields),
        scratch_shapes=[pltpu.VMEM((fields, 3 * rows, width), jnp.float32)],
        compiler_params=pltpu.CompilerParams(vmem_limit_bytes=32 * 1024 * 1024),
    )(low, mid, high, offset, weights)


def spectral_kernel(wave_count, level_count, pair_ref, table_ref, shifted_ref, leg_ref, in_ref, out_ref, lines):
    pair = pair_ref[pl.program_id(0)]
    slots = leg_ref.shape[1]
    half = level_count * GROUP
    legendre = leg_ref[0]
    local_rows = in_ref.shape[1]

    @pl.when(pl.program_id(0) == 0)
    def _():
        tile = lax.broadcasted_iota(jnp.int32, (local_rows, LANES), 1) // (LANES // GROUP)
        for g in range(lines.shape[0]):
            for level in range(level_count):
                parts = [
                    in_ref[(g * GROUP + i) * level_count + level].astype(jnp.float32)
                    for i in range(GROUP)
                ]
                for bit in (1, 2, 4):
                    low_side = (tile & bit) == 0
                    step = bit * (LANES // GROUP)
                    for i in range(GROUP):
                        if i & bit == 0:
                            a, b = parts[i], parts[i + bit]
                            parts[i] = jnp.where(low_side, a, pltpu.roll(b, step, 1))
                            parts[i + bit] = jnp.where(
                                low_side, pltpu.roll(a, LANES - step, 1), b
                            )
                for i in range(GROUP):
                    first = (level * GROUP + i) * local_rows
                    lines[g, first : first + local_rows, :] = parts[i]

    def gathered(which):
        start = 2 * pl.program_id(0) + which
        return jnp.concatenate(
            [lines[g, pl.ds(start, half, stride=local_rows), :] for g in range(lines.shape[0])],
            axis=1,
        )

    stacked = jnp.concatenate([gathered(0), gathered(1)], axis=0).astype(jnp.bfloat16)
    projected = lax.dot_general(
        stacked, legendre, (((1,), (1,)), ((), ())), preferred_element_type=jnp.float32
    )
    table = table_ref[...]
    rolled = pltpu.roll(table, table.shape[1] - pair, 1)[:, :slots]
    upper = shifted_ref[:, :slots]

    def lower_mask(rows):
        return lax.broadcasted_iota(jnp.int32, (rows, slots), 1) < wave_count - pair

    operator = jnp.where(lower_mask(level_count * level_count), rolled, upper)
    mask = lower_mask(half)
    chosen = jnp.where(mask, projected[:half], projected[half:])
    solved = []
    for v in range(level_count):
        total = jnp.zeros((GROUP, slots), jnp.float32)
        for w in range(level_count):
            row = v * level_count + w
            total = total + operator[row : row + 1] * chosen[w * GROUP : (w + 1) * GROUP]
        solved.append(total)
    solved = jnp.concatenate(solved, axis=0)
    placed = jnp.concatenate([jnp.where(mask, solved, 0.0), jnp.where(mask, 0.0, solved)], axis=0)
    returned = jnp.dot(
        placed.astype(jnp.bfloat16), legendre, preferred_element_type=jnp.float32
    )
    out_ref[0] = returned.astype(out_ref.dtype)


def spectral(pair_here, helmholtz, legendre, moved):
    pair_local, slot_count, lat_total = legendre.shape
    wave_count, level_count, _ = helmholtz.shape
    rows = 2 * level_count * GROUP
    span = -(-slot_count // 256) * 256
    flat = helmholtz.reshape(wave_count, level_count * level_count).T
    table = jnp.pad(flat, ((0, 0), (0, span - wave_count)))
    shifted = jnp.pad(flat, ((0, 0), (1, span - wave_count - 1)))
    whole = pl.BlockSpec(table.shape, lambda i, pair: (0, 0))
    return pl.pallas_call(
        functools.partial(spectral_kernel, wave_count, level_count),
        grid_spec=pltpu.PrefetchScalarGridSpec(
            num_scalar_prefetch=1,
            grid=(pair_local,),
            in_specs=[
                whole,
                whole,
                pl.BlockSpec((1, slot_count, lat_total), lambda i, pair: (i, 0, 0)),
                pl.BlockSpec(moved.shape, lambda i, pair: (0, 0, 0)),
            ],
            out_specs=pl.BlockSpec((1, rows, lat_total), lambda i, pair: (i, 0, 0)),
            scratch_shapes=[
                pltpu.VMEM(
                    (lat_total // LANES, level_count * GROUP * moved.shape[1], LANES), jnp.float32
                )
            ],
        ),
        out_shape=jax.ShapeDtypeStruct((pair_local, rows, lat_total), moved.dtype),
        compiler_params=pltpu.CompilerParams(vmem_limit_bytes=32 * 1024 * 1024),
    )(pair_here, table, shifted, legendre, moved)


def shards(grid_old, depart_offset, interp_weights, pair_order, legendre, helmholtz):
    lat_count = lax.axis_size("lat")
    lev_count = lax.axis_size("lev")
    fields, lev_local, row_count, lon_count = grid_old.shape
    pair_count = pair_order.shape[0]
    pair_local, slot_count, lat_total = legendre.shape
    wave_count = helmholtz.shape[0]
    level_count = helmholtz.shape[1]
    local = fields * lev_local * row_count
    quarter = lon_count // 4
    assert row_count >= HMAX and 2 * fields <= GROUP and lev_local == 1
    assert row_count * GROUP == LANES and lat_count % GROUP == 0
    (basis0, basis2, basis_odd), order = tables(lon_count, wave_count)
    count0, count2 = basis0.shape[1], basis2.shape[1]

    forward = [(i, i + 1) for i in range(lat_count - 1)]
    backward = [(i + 1, i) for i in range(lat_count - 1)]
    groups = (fields * (HMAX // EDGE), EDGE, lon_count)
    low = lax.ppermute(grid_old[:, 0, row_count - HMAX :].reshape(groups), "lat", forward)
    high = lax.ppermute(grid_old[:, 0, :HMAX].reshape(groups), "lat", backward)
    arrival = interpolate(low, grid_old[:, 0], high, depart_offset[0], interp_weights[:, 0])
    flat = arrival.reshape(local, lon_count).astype(jnp.float32)
    f0, f1, f2, f3 = [flat[:, a * quarter : (a + 1) * quarter] for a in range(4)]
    even, swing = f0 + f2, f1 + f3
    kind = jnp.bfloat16
    sum0 = (even + swing).astype(kind)
    sum2 = (even - swing).astype(kind)
    odd = jnp.concatenate([(f0 - f2).astype(kind), (f1 - f3).astype(kind)], axis=1)

    def project(basis, part):
        return lax.dot_general(
            basis, part, (((2,), (1,)), ((), ())), preferred_element_type=jnp.float32
        ).astype(kind)

    fourier = jnp.concatenate(
        [project(basis0, sum0), project(basis2, sum2), project(basis_odd, odd)], axis=1
    )
    waves = jnp.stack([pair_order, wave_count - 1 - pair_order], axis=1).reshape(-1)
    match = waves[:, None] == order[None, :]
    select = match.astype(kind)
    sent = jnp.concatenate(
        [
            jnp.dot(select, fourier[c], preferred_element_type=jnp.float32).astype(kind)
            for c in range(2)
        ]
        + [jnp.zeros((2 * pair_count, LANES - 2 * local), kind)],
        axis=1,
    )
    moved = lax.all_to_all(sent, ("lat", "lev"), split_axis=0, concat_axis=0, tiled=True)
    moved = moved.reshape(lat_count * lev_count, 2 * pair_local, LANES)
    holder = lax.axis_index("lat") * lev_count + lax.axis_index("lev")
    pair_here = lax.dynamic_slice_in_dim(pair_order, holder * pair_local, pair_local)
    returned = spectral(pair_here, helmholtz, legendre, moved)
    returned = returned.reshape(pair_local, 2, level_count, GROUP, lat_total)[:, :, :, : 2 * fields]
    returned = returned.reshape(
        pair_local, 2, lev_count, lev_local, 2 * fields, lat_count, row_count
    )
    outgoing = returned.transpose(5, 2, 0, 1, 4, 3, 6).reshape(pair_count * 2, 2 * local)
    arrived = lax.all_to_all(outgoing, ("lat", "lev"), split_axis=0, concat_axis=0, tiled=True)
    gain = jnp.where(match, np.where(order == 0, 1.0, 2.0).astype(np.float32)[None, :], 0.0)
    natural = lax.dot_general(
        gain.astype(kind), arrived, (((0,), (0,)), ((), ())), preferred_element_type=jnp.float32
    ).astype(kind)

    def rebuild(basis, first):
        total = 0.0
        for c in range(2):
            rows = natural[first : first + basis.shape[1], c * local : (c + 1) * local]
            total = total + lax.dot_general(
                rows, basis[c], (((0,), (0,)), ((), ())), preferred_element_type=jnp.float32
            )
        return total

    back0 = rebuild(basis0, 0)
    back2 = rebuild(basis2, count0)
    back_odd = rebuild(basis_odd, count0 + count2)
    plus, minus = back0 + back2, back0 - back2
    left, right = back_odd[:, :quarter], back_odd[:, quarter:]
    rebuilt = jnp.concatenate([plus + left, minus + right, plus - left, minus - right], axis=1)
    return rebuilt.astype(kind).reshape(fields, lev_local, row_count, lon_count)


def solution(mesh):
    in_specs = (
        P(None, "lev", "lat", None),
        P("lev", "lat", None),
        P(None, "lev", "lat", None),
        P(),
        P(("lat", "lev"), None, None),
        P(),
    )
    out_specs = P(None, "lev", "lat", None)
    return jax.shard_map(shards, mesh=mesh, in_specs=in_specs, out_specs=out_specs, check_vma=False)
```

```python
import functools
import math

import jax
import jax.numpy as jnp
import numpy as np
from jax import lax
from jax.experimental import pallas as pl
from jax.experimental.pallas import tpu as pltpu
from jax.sharding import PartitionSpec as P

HMAX = 12
LANES = 128
GROUP = 8
EDGE = 4


@functools.lru_cache(maxsize=None)
def tables(lon_count, wave_count):
    quarter = lon_count // 4
    classes = [np.arange(k, wave_count, 4) for k in (0, 2)]
    odd = np.arange(1, wave_count, 2)
    column = np.arange(quarter)
    norm = 1.0 / math.sqrt(lon_count)
    built = []
    for waves in classes:
        angle = (waves[:, None] * column[None, :] % lon_count) * (2.0 * math.pi / lon_count)
        built.append(np.stack([np.cos(angle), -np.sin(angle)]) * norm)
    angle = (odd[:, None] * column[None, :] % lon_count) * (2.0 * math.pi / lon_count)
    sign = np.where(odd % 4 == 1, 1.0, -1.0)[:, None]
    cos, sin = np.cos(angle), np.sin(angle)
    real = np.concatenate([cos, -sign * sin], axis=1)
    imag = np.concatenate([-sin, -sign * cos], axis=1)
    built.append(np.stack([real, imag]) * norm)
    order = np.concatenate(classes + [odd]).astype(np.int32)
    return [t.astype(np.float32).astype(jnp.bfloat16) for t in built], order


def interp_kernel(low_ref, mid_ref, high_ref, offset_ref, weight_ref, out_ref, wide):
    fields, rows, width = mid_ref.shape
    for f in range(fields):
        wide[f, rows : 2 * rows, :] = mid_ref[f].astype(jnp.float32)
        for first, ref in ((rows - HMAX, low_ref), (2 * rows, high_ref)):
            for g in range(HMAX // EDGE):
                start = first + g * EDGE
                part = ref[f * (HMAX // EDGE) + g]
                wide[f, start : start + EDGE, :] = part.astype(jnp.float32)

    def chunk(step, carry):
        here = pl.ds(pl.multiple_of(step * LANES, LANES), LANES)
        offset = offset_ref[:, here]
        weights = [weight_ref[k, :, here].astype(jnp.float32) for k in range(4)]
        totals = [jnp.zeros((rows, LANES), jnp.float32) for _ in range(fields)]
        picks = [offset == start for start in range(-HMAX, HMAX - 2)]
        for shift in range(-HMAX, HMAX + 1):
            coefficient = jnp.zeros((rows, LANES), jnp.float32)
            for k in range(4):
                start = shift - k
                if -HMAX <= start < HMAX - 2:
                    coefficient = jnp.where(picks[start + HMAX], weights[k], coefficient)
            for f in range(fields):
                totals[f] = totals[f] + coefficient * wide[f, pl.ds(rows + shift, rows), here]
        for f in range(fields):
            out_ref[f, :, here] = totals[f].astype(out_ref.dtype)
        return carry

    lax.fori_loop(0, width // LANES, chunk, 0)


def interpolate(low, mid, high, offset, weights):
    fields, rows, lon_count = mid.shape
    width = lon_count // 4

    def block(lead):
        return pl.BlockSpec((lead, rows, width), lambda i: (0, 0, i))

    edge = pl.BlockSpec((low.shape[0], EDGE, width), lambda i: (0, 0, i))
    return pl.pallas_call(
        interp_kernel,
        grid=(lon_count // width,),
        out_shape=jax.ShapeDtypeStruct(mid.shape, mid.dtype),
        in_specs=[
            edge,
            block(fields),
            edge,
            pl.BlockSpec((rows, width), lambda i: (0, i)),
            block(4),
        ],
        out_specs=block(fields),
        scratch_shapes=[pltpu.VMEM((fields, 3 * rows, width), jnp.float32)],
        compiler_params=pltpu.CompilerParams(vmem_limit_bytes=32 * 1024 * 1024),
    )(low, mid, high, offset, weights)


def exchange(parts, tile):
    for bit in (1, 2, 4):
        low_side = (tile & bit) == 0
        step = bit * (LANES // GROUP)
        for i in range(GROUP):
            if i & bit == 0:
                a, b = parts[i], parts[i + bit]
                parts[i] = jnp.where(low_side, a, pltpu.roll(b, step, 1))
                parts[i + bit] = jnp.where(low_side, pltpu.roll(a, LANES - step, 1), b)


def spectral_kernel(wave_count, level_count, pair_ref, table_ref, shifted_ref, leg_ref, in_ref, out_ref, lines):
    pair = pair_ref[pl.program_id(0)]
    slots = leg_ref.shape[1]
    half = level_count * GROUP
    legendre = leg_ref[0]
    local_rows = in_ref.shape[1]

    @pl.when(pl.program_id(0) == 0)
    def _():
        tile = lax.broadcasted_iota(jnp.int32, (local_rows, LANES), 1) // (LANES // GROUP)
        for g in range(lines.shape[0]):
            for level in range(level_count):
                parts = [
                    in_ref[(g * GROUP + i) * level_count + level].astype(jnp.float32)
                    for i in range(GROUP)
                ]
                exchange(parts, tile)
                for i in range(GROUP):
                    first = (level * GROUP + i) * local_rows
                    lines[g, first : first + local_rows, :] = parts[i]

    def gathered(which):
        start = 2 * pl.program_id(0) + which
        return jnp.concatenate(
            [lines[g, pl.ds(start, half, stride=local_rows), :] for g in range(lines.shape[0])],
            axis=1,
        )

    stacked = jnp.concatenate([gathered(0), gathered(1)], axis=0).astype(jnp.bfloat16)
    projected = lax.dot_general(
        stacked, legendre, (((1,), (1,)), ((), ())), preferred_element_type=jnp.float32
    )
    table = table_ref[...]
    rolled = pltpu.roll(table, table.shape[1] - pair, 1)[:, :slots]
    upper = shifted_ref[:, :slots]

    def lower_mask(rows):
        return lax.broadcasted_iota(jnp.int32, (rows, slots), 1) < wave_count - pair

    operator = jnp.where(lower_mask(level_count * level_count), rolled, upper)
    mask = lower_mask(half)
    chosen = jnp.where(mask, projected[:half], projected[half:])
    solved = []
    for v in range(level_count):
        total = jnp.zeros((GROUP, slots), jnp.float32)
        for w in range(level_count):
            row = v * level_count + w
            total = total + operator[row : row + 1] * chosen[w * GROUP : (w + 1) * GROUP]
        solved.append(total)
    solved = jnp.concatenate(solved, axis=0)
    placed = jnp.concatenate([jnp.where(mask, solved, 0.0), jnp.where(mask, 0.0, solved)], axis=0)
    returned = jnp.dot(
        placed.astype(jnp.bfloat16), legendre, preferred_element_type=jnp.float32
    )
    for which in range(2):
        start = 2 * pl.program_id(0) + which
        for g in range(lines.shape[0]):
            lines[g, pl.ds(start, half, stride=local_rows), :] = returned[
                which * half : (which + 1) * half, g * LANES : (g + 1) * LANES
            ]

    @pl.when(pl.program_id(0) == pl.num_programs(0) - 1)
    def _():
        tile = lax.broadcasted_iota(jnp.int32, (local_rows, LANES), 1) // (LANES // GROUP)
        for g in range(lines.shape[0]):
            for level in range(level_count):
                parts = []
                for i in range(GROUP):
                    first = (level * GROUP + i) * local_rows
                    parts.append(lines[g, first : first + local_rows, :])
                exchange(parts, tile)
                for i in range(GROUP):
                    holder = (g * GROUP + i) * level_count + level
                    out_ref[holder] = parts[i].astype(out_ref.dtype)


def spectral(pair_here, helmholtz, legendre, moved):
    pair_local, slot_count, lat_total = legendre.shape
    wave_count, level_count, _ = helmholtz.shape
    span = -(-slot_count // 256) * 256
    flat = helmholtz.reshape(wave_count, level_count * level_count).T
    table = jnp.pad(flat, ((0, 0), (0, span - wave_count)))
    shifted = jnp.pad(flat, ((0, 0), (1, span - wave_count - 1)))
    whole = pl.BlockSpec(table.shape, lambda i, pair: (0, 0))
    return pl.pallas_call(
        functools.partial(spectral_kernel, wave_count, level_count),
        grid_spec=pltpu.PrefetchScalarGridSpec(
            num_scalar_prefetch=1,
            grid=(pair_local,),
            in_specs=[
                whole,
                whole,
                pl.BlockSpec((1, slot_count, lat_total), lambda i, pair: (i, 0, 0)),
                pl.BlockSpec(moved.shape, lambda i, pair: (0, 0, 0)),
            ],
            out_specs=pl.BlockSpec(moved.shape, lambda i, pair: (0, 0, 0)),
            scratch_shapes=[
                pltpu.VMEM(
                    (lat_total // LANES, level_count * GROUP * moved.shape[1], LANES), jnp.float32
                )
            ],
        ),
        out_shape=jax.ShapeDtypeStruct(moved.shape, moved.dtype),
        compiler_params=pltpu.CompilerParams(vmem_limit_bytes=32 * 1024 * 1024),
    )(pair_here, table, shifted, legendre, moved)


def shards(grid_old, depart_offset, interp_weights, pair_order, legendre, helmholtz):
    lat_count = lax.axis_size("lat")
    lev_count = lax.axis_size("lev")
    fields, lev_local, row_count, lon_count = grid_old.shape
    pair_count = pair_order.shape[0]
    pair_local, slot_count, lat_total = legendre.shape
    wave_count = helmholtz.shape[0]
    level_count = helmholtz.shape[1]
    local = fields * lev_local * row_count
    quarter = lon_count // 4
    assert row_count >= HMAX and 2 * fields <= GROUP and lev_local == 1
    assert row_count * GROUP == LANES and lat_count % GROUP == 0
    (basis0, basis2, basis_odd), order = tables(lon_count, wave_count)
    count0, count2 = basis0.shape[1], basis2.shape[1]

    forward = [(i, i + 1) for i in range(lat_count - 1)]
    backward = [(i + 1, i) for i in range(lat_count - 1)]
    groups = (fields * (HMAX // EDGE), EDGE, lon_count)
    low = lax.ppermute(grid_old[:, 0, row_count - HMAX :].reshape(groups), "lat", forward)
    high = lax.ppermute(grid_old[:, 0, :HMAX].reshape(groups), "lat", backward)
    arrival = interpolate(low, grid_old[:, 0], high, depart_offset[0], interp_weights[:, 0])
    flat = arrival.reshape(local, lon_count).astype(jnp.float32)
    f0, f1, f2, f3 = [flat[:, a * quarter : (a + 1) * quarter] for a in range(4)]
    even, swing = f0 + f2, f1 + f3
    kind = jnp.bfloat16
    sum0 = (even + swing).astype(kind)
    sum2 = (even - swing).astype(kind)
    odd = jnp.concatenate([(f0 - f2).astype(kind), (f1 - f3).astype(kind)], axis=1)

    def project(basis, part):
        return lax.dot_general(
            basis, part, (((2,), (1,)), ((), ())), preferred_element_type=jnp.float32
        ).astype(kind)

    fourier = jnp.concatenate(
        [project(basis0, sum0), project(basis2, sum2), project(basis_odd, odd)], axis=1
    )
    waves = jnp.stack([pair_order, wave_count - 1 - pair_order], axis=1).reshape(-1)
    match = waves[:, None] == order[None, :]
    select = match.astype(kind)
    sent = jnp.concatenate(
        [
            jnp.dot(select, fourier[c], preferred_element_type=jnp.float32).astype(kind)
            for c in range(2)
        ]
        + [jnp.zeros((2 * pair_count, LANES - 2 * local), kind)],
        axis=1,
    )
    moved = lax.all_to_all(sent, ("lat", "lev"), split_axis=0, concat_axis=0, tiled=True)
    moved = moved.reshape(lat_count * lev_count, 2 * pair_local, LANES)
    holder = lax.axis_index("lat") * lev_count + lax.axis_index("lev")
    pair_here = lax.dynamic_slice_in_dim(pair_order, holder * pair_local, pair_local)
    returned = spectral(pair_here, helmholtz, legendre, moved)
    outgoing = returned.reshape(2 * pair_count, LANES)
    arrived = lax.all_to_all(outgoing, ("lat", "lev"), split_axis=0, concat_axis=0, tiled=True)
    gain = jnp.where(match, np.where(order == 0, 1.0, 2.0).astype(np.float32)[None, :], 0.0)
    natural = lax.dot_general(
        gain.astype(kind), arrived, (((0,), (0,)), ((), ())), preferred_element_type=jnp.float32
    ).astype(kind)

    def rebuild(basis, first):
        total = 0.0
        for c in range(2):
            rows = natural[first : first + basis.shape[1], c * local : (c + 1) * local]
            total = total + lax.dot_general(
                rows, basis[c], (((0,), (0,)), ((), ())), preferred_element_type=jnp.float32
            )
        return total

    back0 = rebuild(basis0, 0)
    back2 = rebuild(basis2, count0)
    back_odd = rebuild(basis_odd, count0 + count2)
    plus, minus = back0 + back2, back0 - back2
    left, right = back_odd[:, :quarter], back_odd[:, quarter:]
    rebuilt = jnp.concatenate([plus + left, minus + right, plus - left, minus - right], axis=1)
    return rebuilt.astype(kind).reshape(fields, lev_local, row_count, lon_count)


def solution(mesh):
    in_specs = (
        P(None, "lev", "lat", None),
        P("lev", "lat", None),
        P(None, "lev", "lat", None),
        P(),
        P(("lat", "lev"), None, None),
        P(),
    )
    out_specs = P(None, "lev", "lat", None)
    return jax.shard_map(shards, mesh=mesh, in_specs=in_specs, out_specs=out_specs, check_vma=False)
```

```python
import functools
import math

import jax
import jax.numpy as jnp
import numpy as np
from jax import lax
from jax.experimental import pallas as pl
from jax.experimental.pallas import tpu as pltpu
from jax.sharding import PartitionSpec as P

HMAX = 12
LANES = 128
GROUP = 8
EDGE = 4


@functools.lru_cache(maxsize=None)
def tables(lon_count, wave_count):
    quarter = lon_count // 4
    classes = [np.arange(k, wave_count, 4) for k in (0, 2)]
    odd = np.arange(1, wave_count, 2)
    column = np.arange(quarter)
    norm = 1.0 / math.sqrt(lon_count)
    built = []
    for waves in classes:
        angle = (waves[:, None] * column[None, :] % lon_count) * (2.0 * math.pi / lon_count)
        built.append(np.stack([np.cos(angle), -np.sin(angle)]) * norm)
    angle = (odd[:, None] * column[None, :] % lon_count) * (2.0 * math.pi / lon_count)
    sign = np.where(odd % 4 == 1, 1.0, -1.0)[:, None]
    cos, sin = np.cos(angle), np.sin(angle)
    real = np.concatenate([cos, -sign * sin], axis=1)
    imag = np.concatenate([-sin, -sign * cos], axis=1)
    built.append(np.stack([real, imag]) * norm)
    order = np.concatenate(classes + [odd]).astype(np.int32)
    return [t.astype(np.float32).astype(jnp.bfloat16) for t in built], order


def interp_kernel(low_ref, mid_ref, high_ref, offset_ref, weight_ref, out_ref, wide):
    fields, rows, width = mid_ref.shape
    for f in range(fields):
        wide[f, rows : 2 * rows, :] = mid_ref[f].astype(jnp.float32)
        for first, ref in ((rows - HMAX, low_ref), (2 * rows, high_ref)):
            for g in range(HMAX // EDGE):
                start = first + g * EDGE
                part = ref[f * (HMAX // EDGE) + g]
                wide[f, start : start + EDGE, :] = part.astype(jnp.float32)

    def chunk(step, carry):
        here = pl.ds(pl.multiple_of(step * LANES, LANES), LANES)
        offset = offset_ref[:, here]
        weights = [weight_ref[k, :, here].astype(jnp.float32) for k in range(4)]
        totals = [jnp.zeros((rows, LANES), jnp.float32) for _ in range(fields)]
        picks = {}
        for shift in range(-HMAX, HMAX + 1):
            coefficient = jnp.zeros((rows, LANES), jnp.float32)
            picks[shift] = offset == shift
            for k in range(4):
                start = shift - k
                if -HMAX <= start < HMAX - 2:
                    coefficient = jnp.where(picks[start], weights[k], coefficient)
            for f in range(fields):
                totals[f] = totals[f] + coefficient * wide[f, pl.ds(rows + shift, rows), here]
        for f in range(fields):
            out_ref[f, :, here] = totals[f].astype(out_ref.dtype)
        return carry

    lax.fori_loop(0, width // LANES, chunk, 0, unroll=2)


def interpolate(low, mid, high, offset, weights):
    fields, rows, lon_count = mid.shape
    width = lon_count // 4

    def block(lead):
        return pl.BlockSpec((lead, rows, width), lambda i: (0, 0, i))

    edge = pl.BlockSpec((low.shape[0], EDGE, width), lambda i: (0, 0, i))
    return pl.pallas_call(
        interp_kernel,
        grid=(lon_count // width,),
        out_shape=jax.ShapeDtypeStruct(mid.shape, mid.dtype),
        in_specs=[
            edge,
            block(fields),
            edge,
            pl.BlockSpec((rows, width), lambda i: (0, i)),
            block(4),
        ],
        out_specs=block(fields),
        scratch_shapes=[pltpu.VMEM((fields, 3 * rows, width), jnp.float32)],
        compiler_params=pltpu.CompilerParams(vmem_limit_bytes=32 * 1024 * 1024),
    )(low, mid, high, offset, weights)


def exchange(parts, tile):
    for bit in (1, 2, 4):
        low_side = (tile & bit) == 0
        step = bit * (LANES // GROUP)
        for i in range(GROUP):
            if i & bit == 0:
                a, b = parts[i], parts[i + bit]
                parts[i] = jnp.where(low_side, a, pltpu.roll(b, step, 1))
                parts[i + bit] = jnp.where(low_side, pltpu.roll(a, LANES - step, 1), b)


def spectral_kernel(wave_count, level_count, pair_ref, table_ref, shifted_ref, leg_ref, in_ref, out_ref, lines):
    pair = pair_ref[pl.program_id(0)]
    slots = leg_ref.shape[1]
    half = level_count * GROUP
    legendre = leg_ref[0]
    local_rows = in_ref.shape[1]

    @pl.when(pl.program_id(0) == 0)
    def _():
        tile = lax.broadcasted_iota(jnp.int32, (local_rows, LANES), 1) // (LANES // GROUP)
        for g in range(lines.shape[0]):
            for level in range(level_count):
                parts = [
                    in_ref[(g * GROUP + i) * level_count + level].astype(jnp.float32)
                    for i in range(GROUP)
                ]
                exchange(parts, tile)
                for i in range(GROUP):
                    first = (level * GROUP + i) * local_rows
                    lines[g, first : first + local_rows, :] = parts[i]

    def gathered(which):
        start = 2 * pl.program_id(0) + which
        return jnp.concatenate(
            [lines[g, pl.ds(start, half, stride=local_rows), :] for g in range(lines.shape[0])],
            axis=1,
        )

    stacked = jnp.concatenate([gathered(0), gathered(1)], axis=0).astype(jnp.bfloat16)
    projected = lax.dot_general(
        stacked, legendre, (((1,), (1,)), ((), ())), preferred_element_type=jnp.float32
    )
    table = table_ref[...]
    rolled = pltpu.roll(table, table.shape[1] - pair, 1)[:, :slots]
    upper = shifted_ref[:, :slots]

    def lower_mask(rows):
        return lax.broadcasted_iota(jnp.int32, (rows, slots), 1) < wave_count - pair

    operator = jnp.where(lower_mask(level_count * level_count), rolled, upper)
    mask = lower_mask(half)
    chosen = jnp.where(mask, projected[:half], projected[half:])
    solved = []
    for v in range(level_count):
        total = jnp.zeros((GROUP, slots), jnp.float32)
        for w in range(level_count):
            row = v * level_count + w
            total = total + operator[row : row + 1] * chosen[w * GROUP : (w + 1) * GROUP]
        solved.append(total)
    solved = jnp.concatenate(solved, axis=0)
    placed = jnp.concatenate([jnp.where(mask, solved, 0.0), jnp.where(mask, 0.0, solved)], axis=0)
    returned = jnp.dot(
        placed.astype(jnp.bfloat16), legendre, preferred_element_type=jnp.float32
    )
    for which in range(2):
        start = 2 * pl.program_id(0) + which
        for g in range(lines.shape[0]):
            lines[g, pl.ds(start, half, stride=local_rows), :] = returned[
                which * half : (which + 1) * half, g * LANES : (g + 1) * LANES
            ]

    @pl.when(pl.program_id(0) == pl.num_programs(0) - 1)
    def _():
        tile = lax.broadcasted_iota(jnp.int32, (local_rows, LANES), 1) // (LANES // GROUP)
        for g in range(lines.shape[0]):
            for level in range(level_count):
                parts = []
                for i in range(GROUP):
                    first = (level * GROUP + i) * local_rows
                    parts.append(lines[g, first : first + local_rows, :])
                exchange(parts, tile)
                for i in range(GROUP):
                    holder = (g * GROUP + i) * level_count + level
                    out_ref[holder] = parts[i].astype(out_ref.dtype)


def spectral(pair_here, helmholtz, legendre, moved):
    pair_local, slot_count, lat_total = legendre.shape
    wave_count, level_count, _ = helmholtz.shape
    span = -(-slot_count // 256) * 256
    flat = helmholtz.reshape(wave_count, level_count * level_count).T
    table = jnp.pad(flat, ((0, 0), (0, span - wave_count)))
    shifted = jnp.pad(flat, ((0, 0), (1, span - wave_count - 1)))
    whole = pl.BlockSpec(table.shape, lambda i, pair: (0, 0))
    return pl.pallas_call(
        functools.partial(spectral_kernel, wave_count, level_count),
        grid_spec=pltpu.PrefetchScalarGridSpec(
            num_scalar_prefetch=1,
            grid=(pair_local,),
            in_specs=[
                whole,
                whole,
                pl.BlockSpec((1, slot_count, lat_total), lambda i, pair: (i, 0, 0)),
                pl.BlockSpec(moved.shape, lambda i, pair: (0, 0, 0)),
            ],
            out_specs=pl.BlockSpec(moved.shape, lambda i, pair: (0, 0, 0)),
            scratch_shapes=[
                pltpu.VMEM(
                    (lat_total // LANES, level_count * GROUP * moved.shape[1], LANES), jnp.float32
                )
            ],
        ),
        out_shape=jax.ShapeDtypeStruct(moved.shape, moved.dtype),
        compiler_params=pltpu.CompilerParams(vmem_limit_bytes=32 * 1024 * 1024),
    )(pair_here, table, shifted, legendre, moved)


def shards(grid_old, depart_offset, interp_weights, pair_order, legendre, helmholtz):
    lat_count = lax.axis_size("lat")
    lev_count = lax.axis_size("lev")
    fields, lev_local, row_count, lon_count = grid_old.shape
    pair_count = pair_order.shape[0]
    pair_local, slot_count, lat_total = legendre.shape
    wave_count = helmholtz.shape[0]
    level_count = helmholtz.shape[1]
    local = fields * lev_local * row_count
    quarter = lon_count // 4
    assert row_count >= HMAX and 2 * fields <= GROUP and lev_local == 1
    assert row_count * GROUP == LANES and lat_count % GROUP == 0
    (basis0, basis2, basis_odd), order = tables(lon_count, wave_count)
    count0, count2 = basis0.shape[1], basis2.shape[1]

    forward = [(i, i + 1) for i in range(lat_count - 1)]
    backward = [(i + 1, i) for i in range(lat_count - 1)]
    groups = (fields * (HMAX // EDGE), EDGE, lon_count)
    low = lax.ppermute(grid_old[:, 0, row_count - HMAX :].reshape(groups), "lat", forward)
    high = lax.ppermute(grid_old[:, 0, :HMAX].reshape(groups), "lat", backward)
    arrival = interpolate(low, grid_old[:, 0], high, depart_offset[0], interp_weights[:, 0])
    flat = arrival.reshape(local, lon_count).astype(jnp.float32)
    f0, f1, f2, f3 = [flat[:, a * quarter : (a + 1) * quarter] for a in range(4)]
    even, swing = f0 + f2, f1 + f3
    kind = jnp.bfloat16
    sum0 = (even + swing).astype(kind)
    sum2 = (even - swing).astype(kind)
    odd = jnp.concatenate([(f0 - f2).astype(kind), (f1 - f3).astype(kind)], axis=1)

    def project(basis, part):
        return lax.dot_general(
            basis, part, (((2,), (1,)), ((), ())), preferred_element_type=jnp.float32
        ).astype(kind)

    fourier = jnp.concatenate(
        [project(basis0, sum0), project(basis2, sum2), project(basis_odd, odd)], axis=1
    )
    waves = jnp.stack([pair_order, wave_count - 1 - pair_order], axis=1).reshape(-1)
    match = waves[:, None] == order[None, :]
    select = match.astype(kind)
    sent = jnp.concatenate(
        [
            jnp.dot(select, fourier[c], preferred_element_type=jnp.float32).astype(kind)
            for c in range(2)
        ]
        + [jnp.zeros((2 * pair_count, LANES - 2 * local), kind)],
        axis=1,
    )
    moved = lax.all_to_all(sent, ("lat", "lev"), split_axis=0, concat_axis=0, tiled=True)
    moved = moved.reshape(lat_count * lev_count, 2 * pair_local, LANES)
    holder = lax.axis_index("lat") * lev_count + lax.axis_index("lev")
    pair_here = lax.dynamic_slice_in_dim(pair_order, holder * pair_local, pair_local)
    returned = spectral(pair_here, helmholtz, legendre, moved)
    outgoing = returned.reshape(2 * pair_count, LANES)
    arrived = lax.all_to_all(outgoing, ("lat", "lev"), split_axis=0, concat_axis=0, tiled=True)
    gain = jnp.where(match, np.where(order == 0, 1.0, 2.0).astype(np.float32)[None, :], 0.0)
    natural = lax.dot_general(
        gain.astype(kind), arrived, (((0,), (0,)), ((), ())), preferred_element_type=jnp.float32
    ).astype(kind)

    def rebuild(basis, first):
        total = 0.0
        for c in range(2):
            rows = natural[first : first + basis.shape[1], c * local : (c + 1) * local]
            total = total + lax.dot_general(
                rows, basis[c], (((0,), (0,)), ((), ())), preferred_element_type=jnp.float32
            )
        return total

    back0 = rebuild(basis0, 0)
    back2 = rebuild(basis2, count0)
    back_odd = rebuild(basis_odd, count0 + count2)
    plus, minus = back0 + back2, back0 - back2
    left, right = back_odd[:, :quarter], back_odd[:, quarter:]
    rebuilt = jnp.concatenate([plus + left, minus + right, plus - left, minus - right], axis=1)
    return rebuilt.astype(kind).reshape(fields, lev_local, row_count, lon_count)


def solution(mesh):
    in_specs = (
        P(None, "lev", "lat", None),
        P("lev", "lat", None),
        P(None, "lev", "lat", None),
        P(),
        P(("lat", "lev"), None, None),
        P(),
    )
    out_specs = P(None, "lev", "lat", None)
    return jax.shard_map(shards, mesh=mesh, in_specs=in_specs, out_specs=out_specs, check_vma=False)
```
